512 devices in a mesh: sec: 8 (over z_hi, core), tile: 64 (over x, z_lo, y).
Axes of the slice: x: 4, y: 8, z: 8 (z_hi: 4, z_lo: 2; z = z_hi * 2 + z_lo), core: 2. Of those that a mesh axis runs over, the one named last changes fastest.
Arguments:
- images: bfloat16 [16, 64, 128, 128], P('sec', 'tile'), may hold values from -6 to 6
- pair_skip: int32 [16], P('sec'), may hold values from 1 to 2
- patch_mask: int32 [16, 64, 2], P('sec', 'tile'), may hold values 0 or 1
- cotangent: bfloat16 [16, 64, 2, 128, 128], P('sec', 'tile'), may hold values from -6 to 6
- conv_weight: float32 [4, 9], replicated, may hold values from -2 to 2
- conv_bias: float32 [4], replicated, may hold values from -2 to 2
Outputs:
- feature_grad: float32 [16, 64, 4, 128, 128], P('sec', 'tile')
- weight_grad: float32 [4, 9], replicated
- bias_grad: float32 [4], replicated
The draws below stay inside these ranges and needn't reach their ends.
Inputs may be any that keep to these rules, and one draw needn't show every extreme that they name: Section s is paired with section s + pair_skip[s]; pairs past the last section are dropped.
All inputs are finite; a program needn't handle non-finite values. No bound on the sum of `patch_mask` on one device may be relied on, other than what follows from the above.
Results may differ from the reference program's by a relative error of at most 0.0004.
Values may be sent and summed in bfloat16 or wider, within the bound.
A program may use at most 64 MiB of HBM per device.

```python
import jax
import jax.numpy as jnp
from jax import lax

C = 4
P_SIZE = 128
STRIDE = 64
ROWS = 128
PPS = 2
NSEC = 16
NTILE = 64


def place_ends(result, key, smallest, top_value):
    longest = result.shape.index(max(result.shape))
    spots = []
    for shift in (0, 1):
        where = [jax.random.randint(jax.random.fold_in(key, axis), (), 0, length) for axis, length in enumerate(result.shape)]
        where[longest] = (where[longest] + shift) % result.shape[longest]
        spots.append(tuple(where))
    return result.at[spots[0]].set(smallest).at[spots[1]].set(top_value)


def shard_levels(key, dims, split, smallest, top_value):
    def one(axis_at, shards_of):
        steps = jax.random.uniform(jax.random.fold_in(jax.random.fold_in(key, 6), axis_at), (shards_of,), jnp.float32, smallest / len(split), top_value / len(split))
        return jnp.repeat(jnp.exp(steps), dims[axis_at] // shards_of).reshape((-1,) + (1,) * (len(dims) - axis_at - 1))

    factor_of = one(*split[0])
    for cut in split[1:]:
        factor_of = factor_of * one(*cut)
    return factor_of


def scatter_about(stream_key, shape, deviation, bound, shards=(), kind=jnp.bfloat16):
    result = deviation * jax.random.normal(stream_key, shape, jnp.float32)
    if shards:
        result = result * shard_levels(stream_key, shape, shards, -0.22, 0.18)
    return jnp.clip(result, -bound, bound).astype(kind)


def setup_inputs(seed: int = 0) -> dict:
    key_of = jax.random.split(jax.random.key(seed), 7)
    return {
        "images": scatter_about(key_of[0], (NSEC, NTILE, ROWS, P_SIZE), 1.0, 6.0, ((0, 8), (1, 64))),
        "pair_skip": place_ends(jax.random.randint(key_of[1], (NSEC,), 1, 3), jax.random.fold_in(key_of[1], 1), 1, 2).astype(jnp.int32),
        "patch_mask": place_ends((jax.random.randint(key_of[2], (NSEC, NTILE, PPS), 0, 4) < 3).astype(jnp.int32), jax.random.fold_in(key_of[2], 1), 0, 1),
        "cotangent": scatter_about(key_of[3], (NSEC, NTILE, PPS, P_SIZE, P_SIZE), 1.0, 6.0, ((0, 8), (1, 64))),
        "conv_weight": scatter_about(key_of[4], (C, 9), 9 ** -0.5, 2.0, (), jnp.float32),
        "conv_bias": scatter_about(key_of[5], (C,), 0.5, 2.0, (), jnp.float32),
    }


epsilon = 1e-05

def encode(region, weight, bias):
    height = region.shape[1]
    width = region.shape[2]
    padded = jnp.pad(region, ((0, 0), (0, 2), (0, 2)))
    preact = jnp.zeros((region.shape[0], weight.shape[0], height, width), jnp.float32)
    for row_step in range(3):
        for col_step in range(3):
            preact = preact + weight[:, 3 * row_step + col_step][None, :, None, None] * padded[:, None, row_step:row_step + height, col_step:col_step + width]
    return jnp.tanh(preact + bias[None, :, None, None])

def cut_patches(field):
    channels = field.shape[0]
    padded = jnp.pad(field, ((0, 0), (0, STRIDE), (0, 0)))
    blocks = padded.reshape(channels, padded.shape[1] // STRIDE, STRIDE, padded.shape[2])
    joined = jnp.concatenate([blocks[:, :-1], blocks[:, 1:]], axis=2)
    return joined.transpose(1, 0, 2, 3)

def normalize(patches):
    centered = patches - lax.optimization_barrier(jnp.mean(patches, axis=(2, 3), keepdims=True))
    return centered * lax.rsqrt(lax.optimization_barrier(jnp.sum(centered * centered, axis=(2, 3), keepdims=True)) + epsilon)

def ncc_maps(first, second):
    first_spec = jnp.fft.rfft2(normalize(first))
    second_spec = jnp.fft.rfft2(normalize(second))
    corr = jnp.fft.irfft2(jnp.conj(first_spec) * second_spec, s=(P_SIZE, P_SIZE))
    return lax.optimization_barrier(jnp.mean(corr, axis=1))

def reference(images, pair_skip, patch_mask, cotangent, conv_weight, conv_bias):
    region = images.astype(jnp.float32).reshape(NSEC, NTILE * ROWS, P_SIZE)
    flat_cot = cotangent.astype(jnp.float32).reshape(NSEC, NTILE * PPS, P_SIZE, P_SIZE)
    order = jnp.arange(NSEC, dtype=jnp.int32)
    target = order + pair_skip.astype(jnp.int32)
    inside = (target < NSEC).astype(jnp.float32)
    partner = jnp.minimum(target, NSEC - 1).astype(jnp.int32)
    pair_weights = patch_mask.reshape(NSEC, NTILE * PPS).astype(jnp.float32) * inside[:, None]

    def encoder(weight, bias):
        return encode(region, weight, bias)
    features, pullback = jax.vjp(encoder, conv_weight, conv_bias)

    def total_loss(fields):

        def one_section(section):
            first = cut_patches(fields[section])
            second = cut_patches(fields[partner[section]])
            maps = ncc_maps(first, second)
            return jnp.sum(pair_weights[section][:, None, None] * maps * flat_cot[section])
        return jnp.sum(lax.map(jax.checkpoint(one_section), order))
    feature_grad = jax.grad(total_loss)(features)
    weight_grad, bias_grad = pullback(feature_grad)
    arranged = feature_grad.reshape(NSEC, C, NTILE, ROWS, P_SIZE).transpose(0, 2, 1, 3, 4)
    return (arranged, weight_grad, bias_grad)
```

```python
import functools

import jax
import jax.numpy as jnp
import ml_dtypes
import numpy as np
from jax import lax
from jax.experimental import pallas as pl
from jax.experimental.pallas import tpu as pltpu
from jax.sharding import PartitionSpec as P

MESH = pl.DeviceIdType.MESH
F32 = jnp.float32
BF16 = jnp.bfloat16
SIDE = 128
STEP = 64
EXT = 272
EPS = 1e-5


def dft_constants():
    index = np.arange(SIDE, dtype=np.int64)
    angle = (index[:, None] * index[None, :] % SIDE) * (2.0 * np.pi / SIDE)
    cosine, sine = np.cos(angle), np.sin(angle)
    forward = np.block([[cosine, -sine], [sine, cosine]])
    tables = []
    for table in (forward, forward.T):
        high = table.astype(ml_dtypes.bfloat16)
        low = (table - high.astype(np.float64)).astype(ml_dtypes.bfloat16)
        tables += [high, low]
    return np.stack(tables)


def split(values):
    high = values.astype(BF16)
    return high, (values - high.astype(F32)).astype(BF16)


def dot(left, right):
    return jnp.dot(left, right, preferred_element_type=F32)


def regroup(block):
    top = jnp.concatenate([block[:SIDE, :SIDE], block[SIDE:, :SIDE]], axis=1)
    low = jnp.concatenate([block[:SIDE, SIDE:], block[SIDE:, SIDE:]], axis=1)
    return jnp.concatenate([top, low], axis=0)


def total(block):
    return jnp.sum(jnp.sum(block, axis=0, keepdims=True), axis=1, keepdims=True)


def kernel(
    shape,
    images_hbm,
    cot_hbm,
    tables_hbm,
    skip_ref,
    mask_ref,
    weight_ref,
    bias_ref,
    grad_out,
    wgrad_out,
    bgrad_out,
    own_img,
    own_cot,
    tables,
    imgs,
    cots,
    away,
    flag_out,
    flag_in,
    shifts,
    feat,
    stats,
    kspec,
    cspec,
    gacc,
    acc,
    ring,
    in_sem,
    out_sem,
    send_sem,
    recv_sem,
    ring_send,
    ring_recv,
):
    n_sec, n_tile, n_low = shape
    n_high = n_tile // n_low
    sec = lax.axis_index("sec")
    tile = lax.axis_index("tile")
    low = lax.rem(tile, n_low)
    high = tile // n_low

    def sec_at(step):
        return lax.rem(sec + (step + n_sec), n_sec)

    def tile_at(step):
        return lax.rem(tile + (step + n_tile), n_tile)

    loads = [
        pltpu.make_async_copy(images_hbm, own_img, in_sem.at[0]),
        pltpu.make_async_copy(cot_hbm, own_cot, in_sem.at[1]),
        pltpu.make_async_copy(tables_hbm, tables, in_sem.at[2]),
    ]
    for load in loads:
        load.start()

    around = [(a, b) for a in (-1, 0, 1) for b in (-1, 0, 1) if (a, b) != (0, 0)]
    rings = [
        [(sec_at(d), tile) for d in range(1, n_sec)],
        [(sec, high * n_low + lax.rem(low + d, n_low)) for d in range(1, n_low)],
        [(sec, lax.rem(high + d, n_high) * n_low + low) for d in range(1, n_high)],
    ]
    barrier = pltpu.get_barrier_semaphore()
    for a, b in around:
        pl.semaphore_signal(
            barrier, inc=1, device_id=(sec_at(a), tile_at(b)), device_id_type=MESH
        )
    for group in rings:
        for device in group:
            pl.semaphore_signal(barrier, inc=1, device_id=device, device_id_type=MESH)

    loads[0].wait()
    loads[1].wait()
    skip_even = skip_ref[0]
    skip_odd = skip_ref[1]
    even_next = jnp.where(skip_even == 1, 1.0, 0.0).astype(F32)
    odd_next = jnp.where(skip_odd == 1, 1.0, 0.0).astype(F32)
    flag_out[...] = jnp.full((8, SIDE), odd_next, F32)
    for member in range(2):
        skip = (skip_even, skip_odd)[member]
        target = sec * 2 + member + skip
        inside = jnp.where(target < 2 * n_sec, 1.0, 0.0).astype(F32)
        for anchor in range(2):
            keep = mask_ref[member, anchor].astype(F32) * inside
            weighted = own_cot[member, anchor].astype(F32) * keep
            cots[1, 1 + anchor, member] = weighted.astype(BF16)
            if member == 0:
                weighted = weighted * (1.0 - even_next)
            away[anchor, member] = weighted.astype(BF16)
        imgs[1, member, STEP : STEP + SIDE] = own_img[member]
    pl.semaphore_wait(barrier, len(around) + sum(len(g) for g in rings))

    copies = {}

    def send(name, source, target, device):
        spot = len(copies)
        copy = pltpu.make_async_remote_copy(
            src_ref=source,
            dst_ref=target,
            send_sem=send_sem.at[spot],
            recv_sem=recv_sem.at[spot],
            device_id=device,
            device_id_type=MESH,
        )
        copy.start()
        copies[name] = copy

    down = own_img.at[:, pl.ds(SIDE - STEP, STEP)]
    up = own_img.at[:, pl.ds(0, EXT - SIDE - STEP)]
    top = pl.ds(0, STEP)
    bottom = pl.ds(SIDE + STEP, EXT - SIDE - STEP)
    middle = pl.ds(STEP, SIDE)
    send("down0", down, imgs.at[1, :, top], (sec, tile_at(1)))
    send("up0", up, imgs.at[1, :, bottom], (sec, tile_at(-1)))
    send("cot_t", cots.at[1, 2], cots.at[1, 0], (sec, tile_at(1)))
    send("flag", flag_out, flag_in, (sec_at(1), tile))
    for a in (1, -1):
        send(("mid", a), own_img, imgs.at[1 - a, :, middle], (sec_at(a), tile))
        send(("down", a), down, imgs.at[1 - a, :, top], (sec_at(a), tile_at(1)))
        send(("up", a), up, imgs.at[1 - a, :, bottom], (sec_at(a), tile_at(-1)))
    send("cot_s", away, cots.at[0, pl.ds(1, 2)], (sec_at(1), tile))
    send("cot_d", away.at[1], cots.at[0, 0], (sec_at(1), tile_at(1)))

    first_tile = tile == 0
    last_tile = tile == n_tile - 1
    row_keep = jnp.where(last_tile, 0.0, 1.0).astype(F32)

    loads[2].wait()

    def w_high():
        return tables[0]

    def w_low():
        return tables[1]

    def v_high():
        return tables[2]

    def v_low():
        return tables[3]

    def left_dot(first, second, block):
        hi, lo = split(block)
        return dot(
            jnp.concatenate([first, second, first], axis=1),
            jnp.concatenate([hi, hi, lo], axis=0),
        )

    def right_dot(block, first, second):
        hi, lo = split(block)
        return dot(
            jnp.concatenate([hi, lo, hi], axis=1),
            jnp.concatenate([first, first, second], axis=0),
        )

    def cot_pair(group, anchor):
        both = jnp.concatenate([cots[group, anchor, 0], cots[group, anchor, 1]], axis=0)
        rows = dot(
            jnp.concatenate([both, both], axis=1),
            jnp.concatenate([tables[0, :SIDE], tables[1, :SIDE]], axis=0),
        )
        kspec[group, anchor] = left_dot(v_high(), v_low(), regroup(rows))

    lane = lax.broadcasted_iota(jnp.int32, (EXT, SIDE), 1)
    in_one = jnp.where(lane < SIDE - 1, 1.0, 0.0).astype(F32)
    in_two = jnp.where(lane < SIDE - 2, 1.0, 0.0).astype(F32)

    def encode(slot, image, at):
        shifts[at, 0] = image
        shifts[at, 1] = pltpu.roll(image, SIDE - 1, 1) * in_one
        shifts[at, 2] = pltpu.roll(image, SIDE - 2, 1) * in_two

        def block_of(block, carry):
            start = pl.multiple_of(block * STEP, STEP)
            sums = [jnp.full((STEP, SIDE), bias_ref[c], F32) for c in range(4)]
            for u in range(3):
                for v in range(3):
                    pixels = shifts[at, v, pl.ds(start + u, STEP), :]
                    for c in range(4):
                        sums[c] = sums[c] + weight_ref[c, 3 * u + v] * pixels
            keep = jnp.where(block == 3, row_keep, 1.0)
            means, spreads = [], []
            for c in range(4):
                values = jnp.tanh(sums[c]) * keep
                feat[slot, c, pl.ds(start, STEP), :] = values
                mean = total(values) * (1.0 / (STEP * SIDE))
                away_from = values - mean
                means.append(mean)
                spreads.append(total(away_from * away_from))
            stats[slot, block] = jnp.concatenate(
                [jnp.broadcast_to(s, (1, SIDE)) for s in means + spreads], axis=0
            )
            return carry

        lax.fori_loop(0, 4, block_of, 0)

    def normal(slot, anchor, c):
        first = stats[slot, anchor, pl.ds(c, 1), :]
        second = stats[slot, anchor + 1, pl.ds(c, 1), :]
        apart = first - second
        spread = (
            stats[slot, anchor, pl.ds(4 + c, 1), :]
            + stats[slot, anchor + 1, pl.ds(4 + c, 1), :]
            + (STEP * SIDE // 2) * (apart * apart)
        )
        scale = lax.rsqrt(spread + EPS)
        start = pl.multiple_of(anchor * STEP, STEP)
        values = feat[slot, c, pl.ds(start, SIDE), :]
        return (values - 0.5 * (first + second)) * scale, scale

    def spectrum(slot, anchor):
        n = [normal(slot, anchor, c)[0] for c in range(4)]
        block = jnp.concatenate(
            [jnp.concatenate([n[0], n[1]], axis=1), jnp.concatenate([n[2], n[3]], axis=1)],
            axis=0,
        )
        rows = right_dot(block, w_high(), w_low())
        return left_dot(v_high(), v_low(), regroup(rows))

    def plain_product(k_re, k_im, spec):
        re, im = spec[:SIDE], spec[SIDE:]
        return k_re * re - k_im * im, k_re * im + k_im * re

    def conj_product(k_re, k_im, spec):
        re, im = spec[:SIDE], spec[SIDE:]
        return k_re * re + k_im * im, k_re * im - k_im * re

    def kernel_of(group, anchor, member):
        lanes = pl.ds(member * SIDE, SIDE)
        re = kspec[group, anchor, pl.ds(0, SIDE), lanes]
        im = kspec[group, anchor, pl.ds(SIDE, SIDE), lanes]
        return jnp.concatenate([re, re], axis=1), jnp.concatenate([im, im], axis=1)

    def own_cots(index, carry):
        cot_pair(1, index + 1)
        return carry

    lax.fori_loop(0, 2, own_cots, 0)
    gacc[...] = jnp.zeros_like(gacc)
    acc[...] = jnp.zeros_like(acc)
    for name in ("down0", "up0", "cot_t"):
        copies[name].wait_recv()

    @pl.when(first_tile)
    def _():
        cots[1, 0] = jnp.zeros((2, SIDE, SIDE), BF16)

    @pl.when(last_tile)
    def _():
        imgs[1, :, bottom] = jnp.zeros((2, EXT - SIDE - STEP, SIDE), BF16)

    def own_sections(member, carry):
        encode(member, imgs[1, member].astype(F32), member)
        return carry

    lax.fori_loop(0, 2, own_sections, 0)
    cot_pair(1, 0)

    def own_spectra(anchor, carry):
        cspec[anchor] = spectrum(0, anchor)
        return carry

    lax.fori_loop(0, 3, own_spectra, 0)

    for name in copies:
        if name not in ("down0", "up0", "cot_t"):
            copies[name].wait_recv()

    @pl.when(last_tile)
    def _():
        for side in (0, 2):
            imgs[side, :, bottom] = jnp.zeros((2, EXT - SIDE - STEP, SIDE), BF16)

    @pl.when(first_tile)
    def _():
        cots[0, 0] = jnp.zeros((2, SIDE, SIDE), BF16)

    @pl.when(sec == 0)
    def _():
        cots[0] = jnp.zeros((3, 2, SIDE, SIDE), BF16)

    def prior_sections(member, carry):
        encode(2 + member, imgs[0, member].astype(F32), 2)
        return carry

    lax.fori_loop(0, 2, prior_sections, 0)
    ahead = imgs[2, 0].astype(F32)
    encode(4, even_next * imgs[1, 1].astype(F32) + (1.0 - even_next) * ahead, 2)
    encode(5, odd_next * imgs[2, 0].astype(F32) + (1.0 - odd_next) * imgs[2, 1].astype(F32), 2)

    def anchors(anchor, carry):
        cot_pair(0, anchor)
        came_next = flag_in[0:1, 0:1]
        k_re, k_im = kernel_of(0, anchor, 1)
        last_re, last_im = plain_product(k_re, k_im, spectrum(3, anchor))
        g_re = came_next * last_re
        g_im = came_next * last_im
        h_re = last_re - g_re
        h_im = last_im - g_im
        k_re, k_im = kernel_of(0, anchor, 0)
        p_re, p_im = plain_product(k_re, k_im, spectrum(2, anchor))
        g_re, g_im = g_re + p_re, g_im + p_im
        k_re, k_im = kernel_of(1, anchor, 0)
        p_re, p_im = conj_product(k_re, k_im, spectrum(4, anchor))
        g_re, g_im = g_re + p_re, g_im + p_im
        p_re, p_im = plain_product(k_re, k_im, cspec[anchor])
        h_re, h_im = h_re + even_next * p_re, h_im + even_next * p_im
        k_re, k_im = kernel_of(1, anchor, 1)
        p_re, p_im = conj_product(k_re, k_im, spectrum(5, anchor))
        h_re, h_im = h_re + p_re, h_im + p_im
        for member, (re, im) in enumerate(((g_re, g_im), (h_re, h_im))):
            half = left_dot(w_high(), w_low(), jnp.concatenate([re, im], axis=0))
            back = right_dot(regroup(half), v_high(), v_low())
            for c in range(4):
                q, part = c // 2, c % 2
                slope = back[q * SIDE : (q + 1) * SIDE, part * SIDE : (part + 1) * SIDE]
                slope = slope * (0.25 / (SIDE * SIDE))
                unit, scale = normal(member, anchor, c)
                along = total(slope * unit)
                start = pl.multiple_of(anchor * STEP, STEP)
                gacc[member, c, pl.ds(start, SIDE), :] += scale * (slope - unit * along)
        return carry

    lax.fori_loop(0, 3, anchors, 0)

    results = [
        pltpu.make_async_copy(
            gacc.at[member, :, middle], grad_out.at[member], out_sem.at[member]
        )
        for member in range(2)
    ]
    for result in results:
        result.start()

    def weight_steps(index, carry):
        member = index // 2
        start = pl.multiple_of(STEP + lax.rem(index, 2) * STEP, STEP)
        slopes = []
        for c in range(4):
            values = feat[member, c, pl.ds(start, STEP), :]
            slope = gacc[member, c, pl.ds(start, STEP), :] * (1.0 - values * values)
            slopes.append(slope)
            acc[10 * c + 9] += jnp.sum(slope.reshape(STEP // 8, 8, SIDE), axis=0)
        for u in range(3):
            for v in range(3):
                pixels = shifts[member, v, pl.ds(start + u, STEP), :]
                for c in range(4):
                    part = slopes[c] * pixels
                    acc[10 * c + 3 * u + v] += jnp.sum(part.reshape(STEP // 8, 8, SIDE), axis=0)
        return carry

    lax.fori_loop(0, 4, weight_steps, 0)
    sub8 = lax.broadcasted_iota(jnp.int32, (8, SIDE), 0)
    lane8 = lax.broadcasted_iota(jnp.int32, (8, SIDE), 1)
    mine = jnp.zeros((8, SIDE), F32)
    for tap in range(10):
        for c in range(4):
            spot = (c, tap) if tap < 9 else (4, c)
            here = jnp.logical_and(sub8 == spot[0], lane8 == spot[1])
            mine = mine + jnp.where(here, total(acc[10 * c + tap]), 0.0)

    spots = (sec, low, high)
    sizes = (n_sec, n_low, n_high)
    for stage in range(3):
        spot = spots[stage]
        ring[stage, spot] = mine
        moves = []
        for d in range(1, sizes[stage]):
            copy = pltpu.make_async_remote_copy(
                src_ref=ring.at[stage, spot],
                dst_ref=ring.at[stage, spot],
                send_sem=ring_send.at[stage, d],
                recv_sem=ring_recv.at[stage, d],
                device_id=rings[stage][d - 1],
                device_id_type=MESH,
            )
            copy.start()
            moves.append(copy)
        for copy in moves:
            copy.wait_recv()
        mine = jnp.sum(ring[stage, 0 : sizes[stage]], axis=0)
        for copy in moves:
            copy.wait_send()
    wgrad_out[...] = mine[0:4, 0:9]
    bgrad_out[...] = mine[4:5, 0:4]
    for copy in copies.values():
        copy.wait_send()
    for result in results:
        result.wait()


def on_device(shape, images, pair_skip, patch_mask, cotangent, conv_weight, conv_bias):
    hbm = pl.BlockSpec(memory_space=pl.ANY)
    smem = pl.BlockSpec(memory_space=pltpu.SMEM)
    vmem = pl.BlockSpec(memory_space=pltpu.VMEM)
    wide = max(shape[0], shape[2], shape[1] // shape[2])
    grad, weight_grad, bias_grad = pl.pallas_call(
        functools.partial(kernel, shape),
        out_shape=(
            jax.ShapeDtypeStruct((2, 4, SIDE, SIDE), F32),
            jax.ShapeDtypeStruct((4, 9), F32),
            jax.ShapeDtypeStruct((1, 4), F32),
        ),
        in_specs=[hbm, hbm, hbm, smem, smem, smem, smem],
        out_specs=(hbm, vmem, vmem),
        scratch_shapes=[
            pltpu.VMEM((2, SIDE, SIDE), BF16),
            pltpu.VMEM((2, 2, SIDE, SIDE), BF16),
            pltpu.VMEM((4, 2 * SIDE, 2 * SIDE), BF16),
            pltpu.VMEM((3, 2, EXT, SIDE), BF16),
            pltpu.VMEM((2, 3, 2, SIDE, SIDE), BF16),
            pltpu.VMEM((2, 2, SIDE, SIDE), BF16),
            pltpu.VMEM((8, SIDE), F32),
            pltpu.VMEM((8, SIDE), F32),
            pltpu.VMEM((3, 3, EXT, SIDE), F32),
            pltpu.VMEM((6, 4, 4 * STEP, SIDE), F32),
            pltpu.VMEM((6, 4, 8, SIDE), F32),
            pltpu.VMEM((2, 3, 2 * SIDE, 2 * SIDE), F32),
            pltpu.VMEM((3, 2 * SIDE, 2 * SIDE), F32),
            pltpu.VMEM((2, 4, 4 * STEP, SIDE), F32),
            pltpu.VMEM((40, 8, SIDE), F32),
            pltpu.VMEM((3, wide, 8, SIDE), F32),
            pltpu.SemaphoreType.DMA((3,)),
            pltpu.SemaphoreType.DMA((2,)),
            pltpu.SemaphoreType.DMA((12,)),
            pltpu.SemaphoreType.DMA((12,)),
            pltpu.SemaphoreType.DMA((3, wide)),
            pltpu.SemaphoreType.DMA((3, wide)),
        ],
        compiler_params=pltpu.CompilerParams(
            collective_id=0, has_side_effects=True, vmem_limit_bytes=48 * 1024 * 1024
        ),
    )(
        images[:, 0],
        cotangent[:, 0],
        jnp.asarray(dft_constants()),
        pair_skip,
        patch_mask[:, 0],
        conv_weight,
        conv_bias,
    )
    return grad[:, None], weight_grad, bias_grad[0]


def solution(mesh):
    n_sec, n_tile = mesh.shape["sec"], mesh.shape["tile"]
    n_low = 8 if n_tile % 8 == 0 else 2
    return jax.shard_map(
        functools.partial(on_device, (n_sec, n_tile, n_low)),
        mesh=mesh,
        in_specs=(
            P("sec", "tile", None, None),
            P("sec"),
            P("sec", "tile", None),
            P("sec", "tile", None, None, None),
            P(),
            P(),
        ),
        out_specs=(P("sec", "tile", None, None, None), P(), P()),
        check_vma=False,
    )
```

```python
import functools

import jax
import jax.numpy as jnp
import ml_dtypes
import numpy as np
from jax import lax
from jax.experimental import pallas as pl
from jax.experimental.pallas import tpu as pltpu
from jax.sharding import PartitionSpec as P

MESH = pl.DeviceIdType.MESH
F32 = jnp.float32
BF16 = jnp.bfloat16
SIDE = 128
STEP = 64
EXT = 272
EPS = 1e-5


def dft_constants():
    index = np.arange(SIDE, dtype=np.int64)
    angle = (index[:, None] * index[None, :] % SIDE) * (2.0 * np.pi / SIDE)
    cosine, sine = np.cos(angle), np.sin(angle)
    along = np.block([[cosine, -sine], [sine, cosine]])
    def parts(table):
        high = table.astype(ml_dtypes.bfloat16)
        low = (table - high.astype(np.float64)).astype(ml_dtypes.bfloat16)
        return [high, low]

    return np.stack(parts(along) + parts(along.T))


def split(values):
    high = values.astype(BF16)
    return high, (values - high.astype(F32)).astype(BF16)


def dot(left, right):
    return jnp.dot(left, right, preferred_element_type=F32)


def regroup(block):
    top = jnp.concatenate([block[:SIDE, :SIDE], block[SIDE:, :SIDE]], axis=1)
    low = jnp.concatenate([block[:SIDE, SIDE:], block[SIDE:, SIDE:]], axis=1)
    return jnp.concatenate([top, low], axis=0)


def total(block):
    return jnp.sum(jnp.sum(block, axis=0, keepdims=True), axis=1, keepdims=True)


def kernel(
    shape,
    images_hbm,
    cot_hbm,
    tables_hbm,
    skip_ref,
    mask_ref,
    weight_ref,
    bias_ref,
    grad_out,
    sums_out,
    own_cot,
    tables,
    imgs,
    cots,
    flag_out,
    flag_in,
    band,
    pixels,
    shifts,
    feat,
    stats,
    kspec,
    gspec,
    aspec,
    gacc,
    acc,
    ring,
    in_sem,
    out_sem,
    send_sem,
    recv_sem,
    ring_send,
    ring_recv,
):
    n_sec, n_x, n_z, n_y = shape
    n_tile = n_x * n_z * n_y
    sec = lax.axis_index("sec")
    tile = lax.axis_index("tile")
    at_x = tile // (n_z * n_y)
    at_z = lax.rem(tile // n_y, n_z)
    at_y = lax.rem(tile, n_y)

    def sec_at(step):
        return lax.rem(sec + (step + n_sec), n_sec)

    def tile_at(step):
        return lax.rem(tile + (step + n_tile), n_tile)

    around = [(1, 0), (-1, 0), (0, 1), (0, -1)]
    spots = (sec * n_z + at_z, at_x * n_y + at_y)
    sizes = (n_sec * n_z, n_x * n_y)

    def in_ring(stage, step):
        there = lax.rem(spots[stage] + step, sizes[stage])
        if stage == 0:
            return there // n_z, (at_x * n_z + lax.rem(there, n_z)) * n_y + at_y
        return sec, (there // n_y * n_z + at_z) * n_y + lax.rem(there, n_y)

    rings = [[in_ring(stage, d) for d in range(1, sizes[stage])] for stage in range(2)]
    barrier = pltpu.get_barrier_semaphore()
    for a, b in around:
        pl.semaphore_signal(
            barrier, inc=1, device_id=(sec_at(a), tile_at(b)), device_id_type=MESH
        )
    for group in rings:
        for device in group:
            pl.semaphore_signal(barrier, inc=1, device_id=device, device_id_type=MESH)

    middle = pl.ds(STEP, SIDE)
    loads = [
        pltpu.make_async_copy(images_hbm, imgs.at[1, :, middle], in_sem.at[0]),
        pltpu.make_async_copy(cot_hbm, own_cot, in_sem.at[1]),
        pltpu.make_async_copy(tables_hbm, tables, in_sem.at[2]),
    ]
    for load in loads:
        load.start()
    pl.semaphore_wait(barrier, len(around) + sum(len(g) for g in rings))

    copies = {}

    def send(name, source, target, device):
        spot = len(copies)
        copy = pltpu.make_async_remote_copy(
            src_ref=source,
            dst_ref=target,
            send_sem=send_sem.at[spot],
            recv_sem=recv_sem.at[spot],
            device_id=device,
            device_id_type=MESH,
        )
        copy.start()
        copies[name] = copy

    down = images_hbm.at[:, pl.ds(SIDE - STEP, STEP)]
    up = images_hbm.at[:, pl.ds(0, EXT - SIDE - STEP)]
    top = pl.ds(0, STEP)
    bottom = pl.ds(SIDE + STEP, EXT - SIDE - STEP)
    send("down0", down, imgs.at[1, :, top], (sec, tile_at(1)))
    send("up0", up, imgs.at[1, :, bottom], (sec, tile_at(-1)))
    for a in (1, -1):
        send(("mid", a), images_hbm, imgs.at[1 - a, :, middle], (sec_at(a), tile))

    skip_even = skip_ref[0]
    skip_odd = skip_ref[1]
    even_next = jnp.where(skip_even == 1, 1.0, 0.0).astype(F32)
    odd_next = jnp.where(skip_odd == 1, 1.0, 0.0).astype(F32)
    flag_out[0:1] = jnp.full((1, SIDE), odd_next, F32)
    flag_out[1:2] = jnp.full((1, SIDE), 1.0 - even_next, F32)
    loads[1].wait()
    for member in range(2):
        skip = (skip_even, skip_odd)[member]
        target = sec * 2 + member + skip
        inside = jnp.where(target < 2 * n_sec, 1.0, 0.0).astype(F32)
        for anchor in range(2):
            keep = mask_ref[member, anchor].astype(F32) * inside
            weighted = own_cot[member, anchor].astype(F32) * keep
            cots[1, 1 + anchor, member] = weighted.astype(BF16)
    send("cot_t", cots.at[1, 2], cots.at[1, 0], (sec, tile_at(1)))
    send("flag", flag_out, flag_in, (sec_at(1), tile))
    send("cot_s", cots.at[1, pl.ds(1, 2)], cots.at[0, pl.ds(1, 2)], (sec_at(1), tile))

    first_tile = tile == 0
    last_tile = tile == n_tile - 1
    row_keep = jnp.where(last_tile, 0.0, 1.0).astype(F32)

    def w_high():
        return tables[0]

    def w_low():
        return tables[1]

    def v_high():
        return tables[2]

    def v_low():
        return tables[3]

    def left_dot(first, second, block):
        hi, lo = split(block)
        return dot(
            jnp.concatenate([first, second, first], axis=1),
            jnp.concatenate([hi, hi, lo], axis=0),
        )

    def right_dot(block, first, second):
        hi, lo = split(block)
        return dot(
            jnp.concatenate([hi, lo, hi], axis=1),
            jnp.concatenate([first, first, second], axis=0),
        )

    def cot_pair(group, anchor):
        both = jnp.concatenate([cots[group, anchor, 0], cots[group, anchor, 1]], axis=0)
        rows = dot(
            jnp.concatenate([both, both], axis=1),
            jnp.concatenate([tables[0, :SIDE], tables[1, :SIDE]], axis=0),
        )
        kspec[group, anchor] = left_dot(v_high(), v_low(), regroup(rows))

    apart = lax.broadcasted_iota(jnp.int32, (SIDE, SIDE), 0) - lax.broadcasted_iota(
        jnp.int32, (SIDE, SIDE), 1
    )

    def band_rows(u, carry):
        for c in range(4):
            table = jnp.zeros((SIDE, SIDE), F32)
            for v in range(3):
                table = jnp.where(apart == v, weight_ref[c, 3 * u + v], table)
            hi, lo = split(table)
            lanes = pl.ds(c * SIDE, SIDE)
            band[pl.ds(pl.multiple_of(u * SIDE, SIDE), SIDE), lanes] = hi
            band[pl.ds(pl.multiple_of((3 + u) * SIDE, SIDE), SIDE), lanes] = lo
        return carry

    lane = lax.broadcasted_iota(jnp.int32, (EXT, SIDE), 1)
    in_one = jnp.where(lane < SIDE - 1, 1.0, 0.0).astype(F32)
    in_two = jnp.where(lane < SIDE - 2, 1.0, 0.0).astype(F32)

    def encode(slot, image):
        rows = [image[u : u + 4 * STEP, :].astype(BF16) for u in range(3)]
        sums = dot(jnp.concatenate(rows + rows, axis=1), band[...])
        means, spreads = [], []
        for c in range(4):
            values = jnp.tanh(sums[:, c * SIDE : (c + 1) * SIDE] + bias_ref[c])
            blocks = [values[b * STEP : (b + 1) * STEP] for b in range(4)]
            blocks[3] = blocks[3] * row_keep
            for b in range(4):
                feat[slot, c, b * STEP : (b + 1) * STEP] = blocks[b]
                mean = total(blocks[b]) * (1.0 / (STEP * SIDE))
                means.append(mean)
                off = blocks[b] - mean
                spreads.append(total(off * off))
        for b in range(4):
            stats[slot, b] = jnp.concatenate(
                [jnp.broadcast_to(s, (1, SIDE)) for s in means[b::4] + spreads[b::4]], axis=0
            )

    def normal(slot, anchor, c):
        first = stats[slot, anchor, pl.ds(c, 1), :]
        second = stats[slot, anchor + 1, pl.ds(c, 1), :]
        apart = first - second
        spread = (
            stats[slot, anchor, pl.ds(4 + c, 1), :]
            + stats[slot, anchor + 1, pl.ds(4 + c, 1), :]
            + (STEP * SIDE // 2) * (apart * apart)
        )
        scale = lax.rsqrt(spread + EPS)
        start = anchor * STEP
        values = feat[slot, c, pl.ds(start, SIDE), :]
        return (values - 0.5 * (first + second)) * scale, scale

    def spectrum(slot, anchor):
        n = [normal(slot, anchor, c)[0] for c in range(4)]
        block = jnp.concatenate(
            [jnp.concatenate([n[0], n[1]], axis=1), jnp.concatenate([n[2], n[3]], axis=1)],
            axis=0,
        )
        rows = right_dot(block, w_high(), w_low())
        return left_dot(v_high(), v_low(), regroup(rows))

    def plain_product(k_re, k_im, spec):
        re, im = spec[:SIDE], spec[SIDE:]
        return k_re * re - k_im * im, k_re * im + k_im * re

    def conj_product(k_re, k_im, spec):
        re, im = spec[:SIDE], spec[SIDE:]
        return k_re * re + k_im * im, k_re * im - k_im * re

    def kernel_of(group, anchor, member):
        lanes = pl.ds(member * SIDE, SIDE)
        re = kspec[group, anchor, pl.ds(0, SIDE), lanes]
        im = kspec[group, anchor, pl.ds(SIDE, SIDE), lanes]
        return jnp.concatenate([re, re], axis=1), jnp.concatenate([im, im], axis=1)

    lax.fori_loop(0, 3, band_rows, 0)
    loads[2].wait()
    loads[0].wait()
    def own_cots(index, carry):
        cot_pair(1, index + 1)
        return carry

    lax.fori_loop(0, 2, own_cots, 0)
    gacc[...] = jnp.zeros_like(gacc)
    acc[...] = jnp.zeros_like(acc)
    for name in ("down0", "up0", "cot_t"):
        copies[name].wait_recv()

    @pl.when(first_tile)
    def _():
        cots[1, 0] = jnp.zeros((2, SIDE, SIDE), BF16)

    @pl.when(last_tile)
    def _():
        imgs[1, :, bottom] = jnp.zeros((2, EXT - SIDE - STEP, SIDE), BF16)

    for a in (1, -1):
        for name, rows in (("down", top), ("up", bottom)):
            send((name, a), imgs.at[1, :, rows], imgs.at[1 - a, :, rows], (sec_at(a), tile))
    send("cot_d", cots.at[1, 0], cots.at[0, 0], (sec_at(1), tile))

    def own_sections(member, carry):
        image = imgs[1, member].astype(F32)
        shifts[member, 0] = image
        shifts[member, 1] = pltpu.roll(image, SIDE - 1, 1) * in_one
        shifts[member, 2] = pltpu.roll(image, SIDE - 2, 1) * in_two
        encode(member, shifts.at[member, 0])
        return carry

    lax.fori_loop(0, 2, own_sections, 0)
    cot_pair(1, 0)

    def own_spectra(anchor, carry):
        k_re, k_im = kernel_of(1, anchor, 0)
        re, im = plain_product(k_re, k_im, spectrum(0, anchor))
        gspec[anchor, 0:SIDE] = even_next * re
        gspec[anchor, SIDE:] = even_next * im
        return carry

    lax.fori_loop(0, 3, own_spectra, 0)

    def wait_images(a):
        for name in ("mid", "down", "up"):
            copies[name, a].wait_recv()

    def step(phase, carry):
        before = lax.rem(sec + phase, 2) == 1

        @pl.when(before)
        def _():
            wait_images(1)
            pixels[0] = imgs[0, 0].astype(F32)
            pixels[1] = imgs[0, 1].astype(F32)

        @pl.when(jnp.logical_not(before))
        def _():
            wait_images(-1)
            ahead = imgs[2, 0].astype(F32)
            pixels[2] = even_next * shifts[1, 0] + (1.0 - even_next) * ahead
            pixels[3] = odd_next * ahead + (1.0 - odd_next) * imgs[2, 1].astype(F32)

        base = 2 * lax.rem(sec + phase + 1, 2)
        for i in range(2):
            encode(2 + base + i, pixels.at[base + i])
        for anchor in range(3):
            for i in range(2):
                aspec[base + i, anchor] = spectrum(2 + base + i, anchor)
        return carry

    lax.fori_loop(0, 2, step, 0)

    for name in ("flag", "cot_s", "cot_d"):
        copies[name].wait_recv()

    @pl.when(sec == 0)
    def _():
        cots[0] = jnp.zeros((3, 2, SIDE, SIDE), BF16)

    def finish(anchor):
        cot_pair(0, anchor)
        came_next = flag_in[0:1, 0:1]
        came_after = flag_in[1:2, 0:1]
        k_re, k_im = kernel_of(0, anchor, 1)
        last_re, last_im = plain_product(k_re, k_im, aspec[1, anchor])
        k_re, k_im = kernel_of(0, anchor, 0)
        p_re, p_im = plain_product(came_after * k_re, came_after * k_im, aspec[0, anchor])
        g_re = p_re + came_next * last_re
        g_im = p_im + came_next * last_im
        h_re = gspec[anchor, 0:SIDE] + (1.0 - came_next) * last_re
        h_im = gspec[anchor, SIDE:] + (1.0 - came_next) * last_im
        k_re, k_im = kernel_of(1, anchor, 0)
        p_re, p_im = conj_product(k_re, k_im, aspec[2, anchor])
        g_re, g_im = g_re + p_re, g_im + p_im
        k_re, k_im = kernel_of(1, anchor, 1)
        p_re, p_im = conj_product(k_re, k_im, aspec[3, anchor])
        h_re, h_im = h_re + p_re, h_im + p_im
        for member, (re, im) in enumerate(((g_re, g_im), (h_re, h_im))):
            half = left_dot(w_high(), w_low(), jnp.concatenate([re, im], axis=0))
            back = right_dot(regroup(half), v_high(), v_low())
            for c in range(4):
                q, part = c // 2, c % 2
                slope = back[q * SIDE : (q + 1) * SIDE, part * SIDE : (part + 1) * SIDE]
                slope = slope * (0.25 / (SIDE * SIDE))
                unit, scale = normal(member, anchor, c)
                along = total(slope * unit)
                start = anchor * STEP
                gacc[member, c, pl.ds(start, SIDE), :] += scale * (slope - unit * along)

    for anchor in range(3):
        finish(anchor)

    results = [
        pltpu.make_async_copy(
            gacc.at[member, :, middle], grad_out.at[member], out_sem.at[member]
        )
        for member in range(2)
    ]
    for result in results:
        result.start()

    def weight_steps(index, carry):
        member = index // 2
        start = pl.multiple_of(STEP + lax.rem(index, 2) * STEP, STEP)
        slopes = []
        for c in range(4):
            values = feat[member, c, pl.ds(start, STEP), :]
            slope = gacc[member, c, pl.ds(start, STEP), :] * (1.0 - values * values)
            slopes.append(slope)
            acc[10 * c + 9] += jnp.sum(slope.reshape(STEP // 8, 8, SIDE), axis=0)
        for u in range(3):
            for v in range(3):
                shifted = shifts[member, v, pl.ds(start + u, STEP), :]
                for c in range(4):
                    part = slopes[c] * shifted
                    acc[10 * c + 3 * u + v] += jnp.sum(part.reshape(STEP // 8, 8, SIDE), axis=0)
        return carry

    lax.fori_loop(0, 4, weight_steps, 0)
    place = lax.broadcasted_iota(jnp.int32, (1, SIDE), 1)
    mine = jnp.zeros((1, SIDE), F32)
    for index in range(40):
        mine = mine + jnp.where(place == index, total(acc[index]), 0.0)
    for stage in range(2):
        spot = spots[stage]
        ring[stage, spot] = mine
        moves = []
        for d in range(1, sizes[stage]):
            copy = pltpu.make_async_remote_copy(
                src_ref=ring.at[stage, spot],
                dst_ref=ring.at[stage, spot],
                send_sem=ring_send.at[stage, d],
                recv_sem=ring_recv.at[stage, d],
                device_id=rings[stage][d - 1],
                device_id_type=MESH,
            )
            copy.start()
            moves.append(copy)
        for copy in moves:
            copy.wait_recv()
        mine = jnp.sum(ring[stage, 0 : sizes[stage]], axis=0)
        for copy in moves:
            copy.wait_send()
    sums_out[...] = mine
    for copy in copies.values():
        copy.wait_send()
    for result in results:
        result.wait()


def deliver(grad_ref, sums_ref, grad_out, wgrad_out, bgrad_out):
    grad_out[...] = grad_ref[...]
    sums = jnp.broadcast_to(sums_ref[...], (8, SIDE))
    row = lax.broadcasted_iota(jnp.int32, (8, SIDE), 0)
    place = lax.broadcasted_iota(jnp.int32, (8, SIDE), 1)
    taps = jnp.zeros((8, SIDE), F32)
    biases = jnp.zeros((8, SIDE), F32)
    for c in range(4):
        moved = pltpu.roll(sums, (SIDE - 10 * c) % SIDE, 1)
        taps = jnp.where(row == c, moved, taps)
        moved = pltpu.roll(sums, (SIDE - 10 * c - 9 + c) % SIDE, 1)
        biases = jnp.where(place == c, moved, biases)
    wgrad_out[...] = taps[0:4, 0:9]
    bgrad_out[...] = biases[0:1, 0:4]


def on_device(shape, images, pair_skip, patch_mask, cotangent, conv_weight, conv_bias):
    hbm = pl.BlockSpec(memory_space=pl.ANY)
    smem = pl.BlockSpec(memory_space=pltpu.SMEM)
    vmem = pl.BlockSpec(memory_space=pltpu.VMEM)
    wide = max(shape[0] * shape[2], shape[1] * shape[3])
    held = pl.BlockSpec(memory_space=pltpu.HBM)
    member = pl.BlockSpec((1, 4, SIDE, SIDE), lambda i: (i, 0, 0, 0))
    grad, sums = pl.pallas_call(
        functools.partial(kernel, shape),
        out_shape=(
            jax.ShapeDtypeStruct((2, 4, SIDE, SIDE), F32),
            jax.ShapeDtypeStruct((1, SIDE), F32),
        ),
        in_specs=[held, held, held, smem, smem, smem, smem],
        out_specs=(hbm, vmem),
        scratch_shapes=[
            pltpu.VMEM((2, 2, SIDE, SIDE), BF16),
            pltpu.VMEM((4, 2 * SIDE, 2 * SIDE), BF16),
            pltpu.VMEM((3, 2, EXT, SIDE), BF16),
            pltpu.VMEM((2, 3, 2, SIDE, SIDE), BF16),
            pltpu.VMEM((8, SIDE), F32),
            pltpu.VMEM((8, SIDE), F32),
            pltpu.VMEM((6 * SIDE, 4 * SIDE), BF16),
            pltpu.VMEM((4, EXT, SIDE), F32),
            pltpu.VMEM((2, 3, EXT, SIDE), F32),
            pltpu.VMEM((6, 4, 4 * STEP, SIDE), F32),
            pltpu.VMEM((6, 4, 8, SIDE), F32),
            pltpu.VMEM((2, 3, 2 * SIDE, 2 * SIDE), F32),
            pltpu.VMEM((3, 2 * SIDE, 2 * SIDE), F32),
            pltpu.VMEM((4, 3, 2 * SIDE, 2 * SIDE), F32),
            pltpu.VMEM((2, 4, 4 * STEP, SIDE), F32),
            pltpu.VMEM((40, 8, SIDE), F32),
            pltpu.VMEM((2, wide, 1, SIDE), F32),
            pltpu.SemaphoreType.DMA((3,)),
            pltpu.SemaphoreType.DMA((2,)),
            pltpu.SemaphoreType.DMA((12,)),
            pltpu.SemaphoreType.DMA((12,)),
            pltpu.SemaphoreType.DMA((2, wide)),
            pltpu.SemaphoreType.DMA((2, wide)),
        ],
        compiler_params=pltpu.CompilerParams(
            collective_id=0, has_side_effects=True, vmem_limit_bytes=63 * 1024 * 1024
        ),
    )(
        images[:, 0],
        cotangent[:, 0],
        jnp.asarray(dft_constants()),
        pair_skip,
        patch_mask[:, 0],
        conv_weight,
        conv_bias,
    )
    grad, weight_grad, bias_grad = pl.pallas_call(
        deliver,
        grid=(2,),
        out_shape=(
            jax.ShapeDtypeStruct((2, 4, SIDE, SIDE), F32),
            jax.ShapeDtypeStruct((4, 9), F32),
            jax.ShapeDtypeStruct((1, 4), F32),
        ),
        in_specs=[member, vmem],
        out_specs=(member, vmem, vmem),
    )(grad, sums)
    return grad[:, None], weight_grad, bias_grad[0]


def solution(mesh):
    n_sec, n_tile = mesh.shape["sec"], mesh.shape["tile"]
    sizes = {64: (4, 2, 8), 4: (1, 2, 2)}.get(n_tile, (1, 1, n_tile))
    return jax.shard_map(
        functools.partial(on_device, (n_sec, *sizes)),
        mesh=mesh,
        in_specs=(
            P("sec", "tile", None, None),
            P("sec"),
            P("sec", "tile", None),
            P("sec", "tile", None, None, None),
            P(),
            P(),
        ),
        out_specs=(P("sec", "tile", None, None, None), P(), P()),
        check_vma=False,
    )
```

```python
import functools

import jax
import jax.numpy as jnp
import ml_dtypes
import numpy as np
from jax import lax
from jax.experimental import pallas as pl
from jax.experimental.pallas import tpu as pltpu
from jax.sharding import PartitionSpec as P

MESH = pl.DeviceIdType.MESH
F32 = jnp.float32
BF16 = jnp.bfloat16
SIDE = 128
STEP = 64
EXT = 272
EPS = 1e-5


def dft_constants():
    index = np.arange(SIDE, dtype=np.int64)
    angle = (index[:, None] * index[None, :] % SIDE) * (2.0 * np.pi / SIDE)
    cosine, sine = np.cos(angle), np.sin(angle)
    along = np.block([[cosine, -sine], [sine, cosine]])
    def parts(table):
        high = table.astype(ml_dtypes.bfloat16)
        low = (table - high.astype(np.float64)).astype(ml_dtypes.bfloat16)
        return [high, low]

    return np.stack(parts(along) + parts(along.T))


def split(values):
    high = values.astype(BF16)
    return high, (values - high.astype(F32)).astype(BF16)


def dot(left, right):
    return jnp.dot(left, right, preferred_element_type=F32)


def regroup(block):
    top = jnp.concatenate([block[:SIDE, :SIDE], block[SIDE:, :SIDE]], axis=1)
    low = jnp.concatenate([block[:SIDE, SIDE:], block[SIDE:, SIDE:]], axis=1)
    return jnp.concatenate([top, low], axis=0)


def total(block):
    return jnp.sum(jnp.sum(block, axis=0, keepdims=True), axis=1, keepdims=True)


def kernel(
    shape,
    images_hbm,
    cot_hbm,
    tables_hbm,
    skip_ref,
    mask_ref,
    weight_ref,
    bias_ref,
    grad_out,
    sums_out,
    own_cot,
    tables,
    imgs,
    cots,
    flag_out,
    flag_in,
    band,
    pixels,
    shifts,
    feat,
    stats,
    kspec,
    gspec,
    aspec,
    gacc,
    acc,
    ring,
    in_sem,
    out_sem,
    send_sem,
    recv_sem,
    ring_send,
    ring_recv,
):
    n_sec, n_x, n_z, n_y = shape
    n_tile = n_x * n_z * n_y
    sec = lax.axis_index("sec")
    tile = lax.axis_index("tile")
    at_x = lax.div(tile, n_z * n_y)
    at_z = lax.rem(lax.div(tile, n_y), n_z)
    at_y = lax.rem(tile, n_y)

    def sec_at(step):
        return lax.rem(sec + (step + n_sec), n_sec)

    def tile_at(step):
        return lax.rem(tile + (step + n_tile), n_tile)

    near = sec + 1 - 2 * lax.rem(sec, 2)
    far = lax.rem(sec - 1 + 2 * lax.rem(sec, 2) + n_sec, n_sec)
    around = [(sec, tile_at(1)), (sec, tile_at(-1)), (far, tile), (near, tile)]
    deep = n_sec // 2 * n_z
    at_deep = lax.div(sec, 2) * n_z + at_z
    core = lax.rem(sec, 2)
    spots = (at_deep * 2 + core, at_x * n_y + at_y)

    def hops(step, size):
        return min(step, size - step)

    def in_line(step):
        there = lax.rem(at_deep + step[0], deep)
        other = lax.rem(core + step[1], 2)
        device = (lax.div(there, n_z) * 2 + other, (at_x * n_z + lax.rem(there, n_z)) * n_y + at_y)
        return device

    def in_plane(step):
        to_x, to_y = lax.rem(at_x + step[0], n_x), lax.rem(at_y + step[1], n_y)
        return sec, (to_x * n_z + at_z) * n_y + to_y

    line = [(i, j) for i in range(deep) for j in range(2)][1:]
    plane = [(i, j) for i in range(n_x) for j in range(n_y)][1:]
    line.sort(key=lambda step: -hops(step[0], deep))
    plane.sort(key=lambda step: -hops(step[0], n_x) - hops(step[1], n_y))
    rings = [[in_line(step) for step in line], [in_plane(step) for step in plane]]
    sizes = (deep * 2, n_x * n_y)
    barrier = pltpu.get_barrier_semaphore()
    for device in around:
        pl.semaphore_signal(barrier, inc=1, device_id=device, device_id_type=MESH)
    middle = pl.ds(STEP, SIDE)
    loads = [
        pltpu.make_async_copy(images_hbm, imgs.at[1, :, middle], in_sem.at[0]),
        pltpu.make_async_copy(cot_hbm, own_cot, in_sem.at[1]),
        pltpu.make_async_copy(tables_hbm, tables, in_sem.at[2]),
    ]
    for load in loads:
        load.start()
    for group in rings[::-1]:
        for device in group:
            pl.semaphore_signal(barrier, inc=1, device_id=device, device_id_type=MESH)
    pl.semaphore_wait(barrier, len(around) + sum(len(g) for g in rings))

    copies = {}

    def send(name, source, target, device):
        spot = len(copies)
        copy = pltpu.make_async_remote_copy(
            src_ref=source,
            dst_ref=target,
            send_sem=send_sem.at[spot],
            recv_sem=recv_sem.at[spot],
            device_id=device,
            device_id_type=MESH,
        )
        copy.start()
        copies[name] = copy

    down = images_hbm.at[:, pl.ds(SIDE - STEP, STEP)]
    up = images_hbm.at[:, pl.ds(0, EXT - SIDE - STEP)]
    top = pl.ds(0, STEP)
    bottom = pl.ds(SIDE + STEP, EXT - SIDE - STEP)
    send("down0", down, imgs.at[1, :, top], (sec, tile_at(1)))
    send("up0", up, imgs.at[1, :, bottom], (sec, tile_at(-1)))
    near_slot = 2 * core
    far_slot = 2 - near_slot
    for side, to, slot in (("near", near, near_slot), ("far", far, far_slot)):
        send((side, "mid"), images_hbm, imgs.at[slot, :, middle], (to, tile))

    skip_even = skip_ref[0]
    skip_odd = skip_ref[1]
    even_next = jnp.where(skip_even == 1, 1.0, 0.0).astype(F32)
    odd_next = jnp.where(skip_odd == 1, 1.0, 0.0).astype(F32)
    flag_out[0:1] = jnp.full((1, SIDE), odd_next, F32)
    flag_out[1:2] = jnp.full((1, SIDE), 1.0 - even_next, F32)
    loads[1].wait()
    for member in range(2):
        skip = (skip_even, skip_odd)[member]
        target = sec * 2 + member + skip
        inside = jnp.where(target < 2 * n_sec, 1.0, 0.0).astype(F32)
        for anchor in range(2):
            keep = mask_ref[member, anchor].astype(F32) * inside
            weighted = own_cot[member, anchor].astype(F32) * keep
            cots[1, 1 + anchor, member] = weighted.astype(BF16)
    send("cot_t", cots.at[1, 2], cots.at[1, 0], (sec, tile_at(1)))
    send("flag", flag_out, flag_in, (sec_at(1), tile))
    send("cot_s", cots.at[1, pl.ds(1, 2)], cots.at[0, pl.ds(1, 2)], (sec_at(1), tile))

    first_tile = tile == 0
    last_tile = tile == n_tile - 1
    row_keep = jnp.where(last_tile, 0.0, 1.0).astype(F32)

    def w_high():
        return tables[0]

    def w_low():
        return tables[1]

    def v_high():
        return tables[2]

    def v_low():
        return tables[3]

    def left_dot(first, second, block):
        hi, lo = split(block)
        return dot(
            jnp.concatenate([first, second, first], axis=1),
            jnp.concatenate([hi, hi, lo], axis=0),
        )

    def right_dot(block, first, second):
        hi, lo = split(block)
        return dot(
            jnp.concatenate([hi, lo, hi], axis=1),
            jnp.concatenate([first, first, second], axis=0),
        )

    def cot_pair(group, anchor):
        both = jnp.concatenate([cots[group, anchor, 0], cots[group, anchor, 1]], axis=0)
        rows = dot(
            jnp.concatenate([both, both], axis=1),
            jnp.concatenate([tables[0, :SIDE], tables[1, :SIDE]], axis=0),
        )
        kspec[group, anchor] = left_dot(v_high(), v_low(), regroup(rows))

    apart = lax.broadcasted_iota(jnp.int32, (SIDE, SIDE), 0) - lax.broadcasted_iota(
        jnp.int32, (SIDE, SIDE), 1
    )

    def band_rows(u, carry):
        for c in range(4):
            table = jnp.zeros((SIDE, SIDE), F32)
            for v in range(3):
                table = jnp.where(apart == v, weight_ref[c, 3 * u + v], table)
            hi, lo = split(table)
            lanes = pl.ds(c * SIDE, SIDE)
            band[pl.ds(pl.multiple_of(u * SIDE, SIDE), SIDE), lanes] = hi
            band[pl.ds(pl.multiple_of((3 + u) * SIDE, SIDE), SIDE), lanes] = lo
        return carry

    lane = lax.broadcasted_iota(jnp.int32, (EXT, SIDE), 1)
    in_one = jnp.where(lane < SIDE - 1, 1.0, 0.0).astype(F32)
    in_two = jnp.where(lane < SIDE - 2, 1.0, 0.0).astype(F32)

    def encode(slot, image):
        rows = [image[u : u + 4 * STEP, :].astype(BF16) for u in range(3)]
        sums = dot(jnp.concatenate(rows + rows, axis=1), band[...])
        means, spreads = [], []
        for c in range(4):
            values = jnp.tanh(sums[:, c * SIDE : (c + 1) * SIDE] + bias_ref[c])
            blocks = [values[b * STEP : (b + 1) * STEP] for b in range(4)]
            blocks[3] = blocks[3] * row_keep
            for b in range(4):
                feat[slot, c, b * STEP : (b + 1) * STEP] = blocks[b]
                mean = total(blocks[b]) * (1.0 / (STEP * SIDE))
                means.append(mean)
                off = blocks[b] - mean
                spreads.append(total(off * off))
        for b in range(4):
            stats[slot, b] = jnp.concatenate(
                [jnp.broadcast_to(s, (1, SIDE)) for s in means[b::4] + spreads[b::4]], axis=0
            )

    def normal(slot, anchor, c):
        first = stats[slot, anchor, pl.ds(c, 1), :]
        second = stats[slot, anchor + 1, pl.ds(c, 1), :]
        apart = first - second
        spread = (
            stats[slot, anchor, pl.ds(4 + c, 1), :]
            + stats[slot, anchor + 1, pl.ds(4 + c, 1), :]
            + (STEP * SIDE // 2) * (apart * apart)
        )
        scale = lax.rsqrt(spread + EPS)
        start = anchor * STEP
        values = feat[slot, c, pl.ds(start, SIDE), :]
        return (values - 0.5 * (first + second)) * scale, scale

    def spectrum(slot, anchor):
        n = [normal(slot, anchor, c)[0] for c in range(4)]
        block = jnp.concatenate(
            [jnp.concatenate([n[0], n[1]], axis=1), jnp.concatenate([n[2], n[3]], axis=1)],
            axis=0,
        )
        rows = right_dot(block, w_high(), w_low())
        return left_dot(v_high(), v_low(), regroup(rows))

    def plain_product(k_re, k_im, spec):
        re, im = spec[:SIDE], spec[SIDE:]
        return k_re * re - k_im * im, k_re * im + k_im * re

    def conj_product(k_re, k_im, spec):
        re, im = spec[:SIDE], spec[SIDE:]
        return k_re * re + k_im * im, k_re * im - k_im * re

    def kernel_of(group, anchor, member):
        lanes = pl.ds(member * SIDE, SIDE)
        re = kspec[group, anchor, pl.ds(0, SIDE), lanes]
        im = kspec[group, anchor, pl.ds(SIDE, SIDE), lanes]
        return jnp.concatenate([re, re], axis=1), jnp.concatenate([im, im], axis=1)

    lax.fori_loop(0, 3, band_rows, 0)
    loads[2].wait()
    loads[0].wait()
    def own_cots(index):
        cot_pair(1, index + 1)

    for index in range(2):
        own_cots(index)
    gacc[...] = jnp.zeros_like(gacc)
    acc[...] = jnp.zeros_like(acc)
    for name in ("down0", "up0"):
        copies[name].wait_recv()

    @pl.when(last_tile)
    def _():
        imgs[1, :, bottom] = jnp.zeros((2, EXT - SIDE - STEP, SIDE), BF16)

    for side, to, slot in (("near", near, near_slot), ("far", far, far_slot)):
        for name, rows in (("down", top), ("up", bottom)):
            send((side, name), imgs.at[1, :, rows], imgs.at[slot, :, rows], (to, tile))
    def own_sections(member):
        image = imgs[1, member].astype(F32)
        shifts[member, 0] = image
        shifts[member, 1] = pltpu.roll(image, SIDE - 1, 1) * in_one
        shifts[member, 2] = pltpu.roll(image, SIDE - 2, 1) * in_two
        encode(member, shifts.at[member, 0])

    for index in range(2):
        own_sections(index)
    copies["cot_t"].wait_recv()

    @pl.when(first_tile)
    def _():
        cots[1, 0] = jnp.zeros((2, SIDE, SIDE), BF16)

    send("cot_d", cots.at[1, 0], cots.at[0, 0], (sec_at(1), tile))
    cot_pair(1, 0)

    def own_spectra(anchor):
        k_re, k_im = kernel_of(1, anchor, 0)
        re, im = plain_product(k_re, k_im, spectrum(0, anchor))
        gspec[anchor, 0:SIDE] = even_next * re
        gspec[anchor, SIDE:] = even_next * im

    for index in range(3):
        own_spectra(index)

    def step(phase):
        for name in ("mid", "up", "down"):
            copies[("near", "far")[phase], name].wait_recv()
        base = 2 * phase
        before = lax.rem(sec + phase, 2) == 1

        @pl.when(before)
        def _():
            pixels[base] = imgs[0, 0].astype(F32)
            pixels[base + 1] = imgs[0, 1].astype(F32)

        @pl.when(jnp.logical_not(before))
        def _():
            ahead = imgs[2, 0].astype(F32)
            pixels[base] = even_next * shifts[1, 0] + (1.0 - even_next) * ahead
            pixels[base + 1] = odd_next * ahead + (1.0 - odd_next) * imgs[2, 1].astype(F32)

        for i in range(2):
            encode(2 + base + i, pixels.at[base + i])
        for anchor in range(3):
            for i in range(2):
                aspec[base + i, anchor] = spectrum(2 + base + i, anchor)

    step(0)
    for name in ("flag", "cot_s"):
        copies[name].wait_recv()

    @pl.when(sec == 0)
    def _():
        cots[0, 1:3] = jnp.zeros((2, 2, SIDE, SIDE), BF16)

    def prior_cots(index):
        cot_pair(0, index + 1)

    for index in range(2):
        prior_cots(index)
    step(1)
    copies["cot_d"].wait_recv()

    @pl.when(sec == 0)
    def _():
        cots[0, 0] = jnp.zeros((2, SIDE, SIDE), BF16)

    cot_pair(0, 0)

    prior = 2 - 2 * core
    later = 2 * core

    def finish(anchor):
        came_next = flag_in[0:1, 0:1]
        came_after = flag_in[1:2, 0:1]
        k_re, k_im = kernel_of(0, anchor, 1)
        last_re, last_im = plain_product(k_re, k_im, aspec[prior + 1, anchor])
        k_re, k_im = kernel_of(0, anchor, 0)
        p_re, p_im = plain_product(came_after * k_re, came_after * k_im, aspec[prior, anchor])
        g_re = p_re + came_next * last_re
        g_im = p_im + came_next * last_im
        h_re = gspec[anchor, 0:SIDE] + (1.0 - came_next) * last_re
        h_im = gspec[anchor, SIDE:] + (1.0 - came_next) * last_im
        k_re, k_im = kernel_of(1, anchor, 0)
        p_re, p_im = conj_product(k_re, k_im, aspec[later, anchor])
        g_re, g_im = g_re + p_re, g_im + p_im
        k_re, k_im = kernel_of(1, anchor, 1)
        p_re, p_im = conj_product(k_re, k_im, aspec[later + 1, anchor])
        h_re, h_im = h_re + p_re, h_im + p_im
        for member, (re, im) in enumerate(((g_re, g_im), (h_re, h_im))):
            half = left_dot(w_high(), w_low(), jnp.concatenate([re, im], axis=0))
            back = right_dot(regroup(half), v_high(), v_low())
            for c in range(4):
                q, part = c // 2, c % 2
                slope = back[q * SIDE : (q + 1) * SIDE, part * SIDE : (part + 1) * SIDE]
                slope = slope * (0.25 / (SIDE * SIDE))
                unit, scale = normal(member, anchor, c)
                along = total(slope * unit)
                start = anchor * STEP
                gacc[member, c, pl.ds(start, SIDE), :] += scale * (slope - unit * along)

    def weight_steps(member, half):
        start = STEP + half * STEP
        slopes = []
        for c in range(4):
            values = feat[member, c, pl.ds(start, STEP), :]
            slope = gacc[member, c, pl.ds(start, STEP), :] * (1.0 - values * values)
            slopes.append(slope)
            acc[10 * c + 9] += jnp.sum(slope.reshape(STEP // 8, 8, SIDE), axis=0)
        for u in range(3):
            for v in range(3):
                shifted = shifts[member, v, pl.ds(start + u, STEP), :]
                for c in range(4):
                    part = slopes[c] * shifted
                    acc[10 * c + 3 * u + v] += jnp.sum(part.reshape(STEP // 8, 8, SIDE), axis=0)

    finish(0)
    finish(1)
    weight_steps(0, 0)
    weight_steps(1, 0)
    finish(2)
    results = [
        pltpu.make_async_copy(
            gacc.at[member, :, middle], grad_out.at[member], out_sem.at[member]
        )
        for member in range(2)
    ]
    for result in results:
        result.start()

    weight_steps(0, 1)
    weight_steps(1, 1)
    place = lax.broadcasted_iota(jnp.int32, (1, SIDE), 1)
    mine = jnp.zeros((1, SIDE), F32)
    for index in range(40):
        mine = mine + jnp.where(place == index, total(acc[index]), 0.0)
    for stage in range(2):
        spot = spots[stage]
        ring[stage, spot] = mine
        moves = []
        for d in range(1, sizes[stage]):
            copy = pltpu.make_async_remote_copy(
                src_ref=ring.at[stage, spot],
                dst_ref=ring.at[stage, spot],
                send_sem=ring_send.at[stage, d],
                recv_sem=ring_recv.at[stage, d],
                device_id=rings[stage][d - 1],
                device_id_type=MESH,
            )
            copy.start()
            moves.append(copy)
        for copy in moves:
            copy.wait_recv()
        mine = jnp.sum(ring[stage, 0 : sizes[stage]], axis=0)
        for copy in moves:
            copy.wait_send()
    sums_out[...] = mine
    for copy in copies.values():
        copy.wait_send()
    for result in results:
        result.wait()


def deliver(grad_ref, sums_ref, grad_out, wgrad_out, bgrad_out):
    grad_out[...] = grad_ref[...]
    sums = jnp.broadcast_to(sums_ref[...], (8, SIDE))
    row = lax.broadcasted_iota(jnp.int32, (8, SIDE), 0)
    place = lax.broadcasted_iota(jnp.int32, (8, SIDE), 1)
    taps = jnp.zeros((8, SIDE), F32)
    biases = jnp.zeros((8, SIDE), F32)
    for c in range(4):
        moved = pltpu.roll(sums, (SIDE - 10 * c) % SIDE, 1)
        taps = jnp.where(row == c, moved, taps)
        moved = pltpu.roll(sums, (SIDE - 10 * c - 9 + c) % SIDE, 1)
        biases = jnp.where(place == c, moved, biases)
    wgrad_out[...] = taps[0:4, 0:9]
    bgrad_out[...] = biases[0:1, 0:4]


def on_device(shape, images, pair_skip, patch_mask, cotangent, conv_weight, conv_bias):
    hbm = pl.BlockSpec(memory_space=pl.ANY)
    smem = pl.BlockSpec(memory_space=pltpu.SMEM)
    vmem = pl.BlockSpec(memory_space=pltpu.VMEM)
    wide = max(shape[0] * shape[2], shape[1] * shape[3])
    held = pl.BlockSpec(memory_space=pltpu.HBM)
    member = pl.BlockSpec((1, 4, SIDE, SIDE), lambda i: (i, 0, 0, 0))
    grad, sums = pl.pallas_call(
        functools.partial(kernel, shape),
        out_shape=(
            jax.ShapeDtypeStruct((2, 4, SIDE, SIDE), F32),
            jax.ShapeDtypeStruct((1, SIDE), F32),
        ),
        in_specs=[held, held, held, smem, smem, smem, smem],
        out_specs=(hbm, vmem),
        scratch_shapes=[
            pltpu.VMEM((2, 2, SIDE, SIDE), BF16),
            pltpu.VMEM((4, 2 * SIDE, 2 * SIDE), BF16),
            pltpu.VMEM((3, 2, EXT, SIDE), BF16),
            pltpu.VMEM((2, 3, 2, SIDE, SIDE), BF16),
            pltpu.VMEM((8, SIDE), F32),
            pltpu.VMEM((8, SIDE), F32),
            pltpu.VMEM((6 * SIDE, 4 * SIDE), BF16),
            pltpu.VMEM((4, EXT, SIDE), F32),
            pltpu.VMEM((2, 3, EXT, SIDE), F32),
            pltpu.VMEM((6, 4, 4 * STEP, SIDE), F32),
            pltpu.VMEM((6, 4, 8, SIDE), F32),
            pltpu.VMEM((2, 3, 2 * SIDE, 2 * SIDE), F32),
            pltpu.VMEM((3, 2 * SIDE, 2 * SIDE), F32),
            pltpu.VMEM((4, 3, 2 * SIDE, 2 * SIDE), F32),
            pltpu.VMEM((2, 4, 4 * STEP, SIDE), F32),
            pltpu.VMEM((40, 8, SIDE), F32),
            pltpu.VMEM((2, wide, 1, SIDE), F32),
            pltpu.SemaphoreType.DMA((3,)),
            pltpu.SemaphoreType.DMA((2,)),
            pltpu.SemaphoreType.DMA((12,)),
            pltpu.SemaphoreType.DMA((12,)),
            pltpu.SemaphoreType.DMA((2, wide)),
            pltpu.SemaphoreType.DMA((2, wide)),
        ],
        compiler_params=pltpu.CompilerParams(
            collective_id=0, has_side_effects=True, vmem_limit_bytes=63 * 1024 * 1024
        ),
    )(
        images[:, 0],
        cotangent[:, 0],
        jnp.asarray(dft_constants()),
        pair_skip,
        patch_mask[:, 0],
        conv_weight,
        conv_bias,
    )
    grad, weight_grad, bias_grad = pl.pallas_call(
        deliver,
        grid=(2,),
        out_shape=(
            jax.ShapeDtypeStruct((2, 4, SIDE, SIDE), F32),
            jax.ShapeDtypeStruct((4, 9), F32),
            jax.ShapeDtypeStruct((1, 4), F32),
        ),
        in_specs=[member, vmem],
        out_specs=(member, vmem, vmem),
    )(grad, sums)
    return grad[:, None], weight_grad, bias_grad[0]


def solution(mesh):
    n_sec, n_tile = mesh.shape["sec"], mesh.shape["tile"]
    sizes = {64: (4, 2, 8), 4: (1, 2, 2)}.get(n_tile, (1, 1, n_tile))
    return jax.shard_map(
        functools.partial(on_device, (n_sec, *sizes)),
        mesh=mesh,
        in_specs=(
            P("sec", "tile", None, None),
            P("sec"),
            P("sec", "tile", None),
            P("sec", "tile", None, None, None),
            P(),
            P(),
        ),
        out_specs=(P("sec", "tile", None, None, None), P(), P()),
        check_vma=False,
    )
```

```python
import functools

import jax
import jax.numpy as jnp
import ml_dtypes
import numpy as np
from jax import lax
from jax.experimental import pallas as pl
from jax.experimental.pallas import tpu as pltpu
from jax.sharding import PartitionSpec as P

MESH = pl.DeviceIdType.MESH
F32 = jnp.float32
BF16 = jnp.bfloat16
SIDE = 128
STEP = 64
EXT = 272
EPS = 1e-5


def dft_constants():
    index = np.arange(SIDE, dtype=np.int64)
    angle = (index[:, None] * index[None, :] % SIDE) * (2.0 * np.pi / SIDE)
    cosine, sine = np.cos(angle), np.sin(angle)
    along = np.block([[cosine, -sine], [sine, cosine]])
    def parts(table):
        high = table.astype(ml_dtypes.bfloat16)
        low = (table - high.astype(np.float64)).astype(ml_dtypes.bfloat16)
        return [high, low]

    return np.stack(parts(along) + parts(along.T))


def split(values):
    high = values.astype(BF16)
    return high, (values - high.astype(F32)).astype(BF16)


def dot(left, right):
    return jnp.dot(left, right, preferred_element_type=F32)


def regroup(block):
    top = jnp.concatenate([block[:SIDE, :SIDE], block[SIDE:, :SIDE]], axis=1)
    low = jnp.concatenate([block[:SIDE, SIDE:], block[SIDE:, SIDE:]], axis=1)
    return jnp.concatenate([top, low], axis=0)


def total(block):
    return jnp.sum(jnp.sum(block, axis=0, keepdims=True), axis=1, keepdims=True)


def kernel(
    shape,
    images_hbm,
    cot_hbm,
    tables_hbm,
    skip_hbm,
    mask_hbm,
    weight_hbm,
    bias_hbm,
    grad_out,
    sums_out,
    skip_ref,
    mask_ref,
    weight_ref,
    bias_ref,
    own_cot,
    tables,
    imgs,
    cots,
    flag_out,
    flag_in,
    band,
    pixels,
    shifts,
    feat,
    stats,
    kspec,
    gspec,
    aspec,
    gacc,
    acc,
    ring,
    in_sem,
    out_sem,
    send_sem,
    recv_sem,
    ring_send,
    ring_recv,
):
    n_sec, n_x, n_z, n_y = shape
    n_tile = n_x * n_z * n_y
    sec = lax.axis_index("sec")
    tile = lax.axis_index("tile")
    at_x = lax.div(tile, n_z * n_y)
    at_z = lax.rem(lax.div(tile, n_y), n_z)
    at_y = lax.rem(tile, n_y)

    def sec_at(step):
        return lax.rem(sec + (step + n_sec), n_sec)

    def tile_at(step):
        return lax.rem(tile + (step + n_tile), n_tile)

    near = sec + 1 - 2 * lax.rem(sec, 2)
    far = lax.rem(sec - 1 + 2 * lax.rem(sec, 2) + n_sec, n_sec)
    around = [(sec, tile_at(1)), (sec, tile_at(-1)), (far, tile), (near, tile)]
    deep = n_sec // 2 * n_z
    at_deep = lax.div(sec, 2) * n_z + at_z
    core = lax.rem(sec, 2)
    spots = (at_deep * 2 + core, at_x * n_y + at_y)

    def hops(step, size):
        return min(step, size - step)

    def in_line(step):
        there = lax.rem(at_deep + step[0], deep)
        other = lax.rem(core + step[1], 2)
        device = (lax.div(there, n_z) * 2 + other, (at_x * n_z + lax.rem(there, n_z)) * n_y + at_y)
        return device

    def in_plane(step):
        to_x, to_y = lax.rem(at_x + step[0], n_x), lax.rem(at_y + step[1], n_y)
        return sec, (to_x * n_z + at_z) * n_y + to_y

    line = [(i, j) for i in range(deep) for j in range(2)][1:]
    plane = [(i, j) for i in range(n_x) for j in range(n_y)][1:]
    line.sort(key=lambda step: -hops(step[0], deep))
    plane.sort(key=lambda step: -hops(step[0], n_x) - hops(step[1], n_y))
    rings = [[in_line(step) for step in line], [in_plane(step) for step in plane]]
    sizes = (deep * 2, n_x * n_y)
    barrier = pltpu.get_barrier_semaphore()
    for device in around:
        pl.semaphore_signal(barrier, inc=1, device_id=device, device_id_type=MESH)
    middle = pl.ds(STEP, SIDE)
    loads = [
        pltpu.make_async_copy(images_hbm, imgs.at[1, :, middle], in_sem.at[0]),
        pltpu.make_async_copy(cot_hbm, own_cot, in_sem.at[1]),
        pltpu.make_async_copy(tables_hbm, tables, in_sem.at[2]),
        pltpu.make_async_copy(skip_hbm, skip_ref, in_sem.at[3]),
        pltpu.make_async_copy(mask_hbm, mask_ref, in_sem.at[4]),
        pltpu.make_async_copy(weight_hbm, weight_ref, in_sem.at[5]),
        pltpu.make_async_copy(bias_hbm, bias_ref, in_sem.at[6]),
    ]
    for load in loads:
        load.start()
    for group in rings[::-1]:
        for device in group:
            pl.semaphore_signal(barrier, inc=1, device_id=device, device_id_type=MESH)
    pl.semaphore_wait(barrier, len(around) + sum(len(g) for g in rings))

    copies = {}

    def send(name, source, target, device):
        spot = len(copies)
        copy = pltpu.make_async_remote_copy(
            src_ref=source,
            dst_ref=target,
            send_sem=send_sem.at[spot],
            recv_sem=recv_sem.at[spot],
            device_id=device,
            device_id_type=MESH,
        )
        copy.start()
        copies[name] = copy

    down = images_hbm.at[:, pl.ds(SIDE - STEP, STEP)]
    up = images_hbm.at[:, pl.ds(0, EXT - SIDE - STEP)]
    top = pl.ds(0, STEP)
    bottom = pl.ds(SIDE + STEP, EXT - SIDE - STEP)
    send("down0", down, imgs.at[1, :, top], (sec, tile_at(1)))
    send("up0", up, imgs.at[1, :, bottom], (sec, tile_at(-1)))
    near_slot = 2 * core
    far_slot = 2 - near_slot
    for side, to, slot in (("near", near, near_slot), ("far", far, far_slot)):
        send((side, "mid"), images_hbm, imgs.at[slot, :, middle], (to, tile))

    for load in loads[3:]:
        load.wait()
    skip_even = skip_ref[0]
    skip_odd = skip_ref[1]
    even_next = jnp.where(skip_even == 1, 1.0, 0.0).astype(F32)
    odd_next = jnp.where(skip_odd == 1, 1.0, 0.0).astype(F32)
    flag_out[0:1] = jnp.full((1, SIDE), odd_next, F32)
    flag_out[1:2] = jnp.full((1, SIDE), 1.0 - even_next, F32)
    loads[1].wait()
    for member in range(2):
        skip = (skip_even, skip_odd)[member]
        target = sec * 2 + member + skip
        inside = jnp.where(target < 2 * n_sec, 1.0, 0.0).astype(F32)
        for anchor in range(2):
            keep = mask_ref[member, anchor].astype(F32) * inside
            weighted = own_cot[member, anchor].astype(F32) * keep
            cots[1, 1 + anchor, member] = weighted.astype(BF16)
    send("cot_t", cots.at[1, 2], cots.at[1, 0], (sec, tile_at(1)))
    send("flag", flag_out, flag_in, (sec_at(1), tile))
    send("cot_s", cots.at[1, pl.ds(1, 2)], cots.at[0, pl.ds(1, 2)], (sec_at(1), tile))

    first_tile = tile == 0
    last_tile = tile == n_tile - 1
    row_keep = jnp.where(last_tile, 0.0, 1.0).astype(F32)

    def w_high():
        return tables[0]

    def w_low():
        return tables[1]

    def v_high():
        return tables[2]

    def v_low():
        return tables[3]

    def left_dot(first, second, block):
        hi, lo = split(block)
        return dot(
            jnp.concatenate([first, second, first], axis=1),
            jnp.concatenate([hi, hi, lo], axis=0),
        )

    def right_dot(block, first, second):
        hi, lo = split(block)
        return dot(
            jnp.concatenate([hi, lo, hi], axis=1),
            jnp.concatenate([first, first, second], axis=0),
        )

    def cot_pair(group, anchor):
        both = jnp.concatenate([cots[group, anchor, 0], cots[group, anchor, 1]], axis=0)
        rows = dot(
            jnp.concatenate([both, both], axis=1),
            jnp.concatenate([tables[0, :SIDE], tables[1, :SIDE]], axis=0),
        )
        kspec[group, anchor] = left_dot(v_high(), v_low(), regroup(rows))

    apart = lax.broadcasted_iota(jnp.int32, (SIDE, SIDE), 0) - lax.broadcasted_iota(
        jnp.int32, (SIDE, SIDE), 1
    )

    def band_rows(u, carry):
        for c in range(4):
            table = jnp.zeros((SIDE, SIDE), F32)
            for v in range(3):
                table = jnp.where(apart == v, weight_ref[c, 3 * u + v], table)
            hi, lo = split(table)
            lanes = pl.ds(c * SIDE, SIDE)
            band[pl.ds(pl.multiple_of(u * SIDE, SIDE), SIDE), lanes] = hi
            band[pl.ds(pl.multiple_of((3 + u) * SIDE, SIDE), SIDE), lanes] = lo
        return carry

    lane = lax.broadcasted_iota(jnp.int32, (EXT, SIDE), 1)
    in_one = jnp.where(lane < SIDE - 1, 1.0, 0.0).astype(F32)
    in_two = jnp.where(lane < SIDE - 2, 1.0, 0.0).astype(F32)

    def encode(slot, image):
        rows = [image[u : u + 4 * STEP, :].astype(BF16) for u in range(3)]
        sums = dot(jnp.concatenate(rows + rows, axis=1), band[...])
        means, spreads = [], []
        for c in range(4):
            values = jnp.tanh(sums[:, c * SIDE : (c + 1) * SIDE] + bias_ref[c])
            blocks = [values[b * STEP : (b + 1) * STEP] for b in range(4)]
            blocks[3] = blocks[3] * row_keep
            for b in range(4):
                feat[slot, c, b * STEP : (b + 1) * STEP] = blocks[b]
                mean = total(blocks[b]) * (1.0 / (STEP * SIDE))
                means.append(mean)
                off = blocks[b] - mean
                spreads.append(total(off * off))
        for b in range(4):
            stats[slot, b] = jnp.concatenate(
                [jnp.broadcast_to(s, (1, SIDE)) for s in means[b::4] + spreads[b::4]], axis=0
            )

    def normal(slot, anchor, c):
        first = stats[slot, anchor, pl.ds(c, 1), :]
        second = stats[slot, anchor + 1, pl.ds(c, 1), :]
        apart = first - second
        spread = (
            stats[slot, anchor, pl.ds(4 + c, 1), :]
            + stats[slot, anchor + 1, pl.ds(4 + c, 1), :]
            + (STEP * SIDE // 2) * (apart * apart)
        )
        scale = lax.rsqrt(spread + EPS)
        start = anchor * STEP
        values = feat[slot, c, pl.ds(start, SIDE), :]
        return (values - 0.5 * (first + second)) * scale, scale

    def spectrum(slot, anchor):
        n = [normal(slot, anchor, c)[0] for c in range(4)]
        block = jnp.concatenate(
            [jnp.concatenate([n[0], n[1]], axis=1), jnp.concatenate([n[2], n[3]], axis=1)],
            axis=0,
        )
        rows = right_dot(block, w_high(), w_low())
        return left_dot(v_high(), v_low(), regroup(rows))

    def plain_product(k_re, k_im, spec):
        re, im = spec[:SIDE], spec[SIDE:]
        return k_re * re - k_im * im, k_re * im + k_im * re

    def conj_product(k_re, k_im, spec):
        re, im = spec[:SIDE], spec[SIDE:]
        return k_re * re + k_im * im, k_re * im - k_im * re

    def kernel_of(group, anchor, member):
        lanes = pl.ds(member * SIDE, SIDE)
        re = kspec[group, anchor, pl.ds(0, SIDE), lanes]
        im = kspec[group, anchor, pl.ds(SIDE, SIDE), lanes]
        return jnp.concatenate([re, re], axis=1), jnp.concatenate([im, im], axis=1)

    lax.fori_loop(0, 3, band_rows, 0)
    loads[2].wait()
    loads[0].wait()
    def own_cots(index):
        cot_pair(1, index + 1)

    for index in range(2):
        own_cots(index)
    gacc[...] = jnp.zeros_like(gacc)
    acc[...] = jnp.zeros_like(acc)
    for name in ("down0", "up0"):
        copies[name].wait_recv()

    @pl.when(last_tile)
    def _():
        imgs[1, :, bottom] = jnp.zeros((2, EXT - SIDE - STEP, SIDE), BF16)

    for side, to, slot in (("near", near, near_slot), ("far", far, far_slot)):
        for name, rows in (("down", top), ("up", bottom)):
            send((side, name), imgs.at[1, :, rows], imgs.at[slot, :, rows], (to, tile))
    def own_sections(member):
        image = imgs[1, member].astype(F32)
        shifts[member, 0] = image
        shifts[member, 1] = pltpu.roll(image, SIDE - 1, 1) * in_one
        shifts[member, 2] = pltpu.roll(image, SIDE - 2, 1) * in_two
        encode(member, shifts.at[member, 0])

    for index in range(2):
        own_sections(index)
    copies["cot_t"].wait_recv()

    @pl.when(first_tile)
    def _():
        cots[1, 0] = jnp.zeros((2, SIDE, SIDE), BF16)

    send("cot_d", cots.at[1, 0], cots.at[0, 0], (sec_at(1), tile))
    cot_pair(1, 0)

    def own_spectra(anchor):
        k_re, k_im = kernel_of(1, anchor, 0)
        re, im = plain_product(k_re, k_im, spectrum(0, anchor))
        gspec[anchor, 0:SIDE] = even_next * re
        gspec[anchor, SIDE:] = even_next * im

    for index in range(3):
        own_spectra(index)

    def step(phase):
        for name in ("mid", "up", "down"):
            copies[("near", "far")[phase], name].wait_recv()
        base = 2 * phase
        before = lax.rem(sec + phase, 2) == 1

        @pl.when(before)
        def _():
            pixels[base] = imgs[0, 0].astype(F32)
            pixels[base + 1] = imgs[0, 1].astype(F32)

        @pl.when(jnp.logical_not(before))
        def _():
            ahead = imgs[2, 0].astype(F32)
            pixels[base] = even_next * shifts[1, 0] + (1.0 - even_next) * ahead
            pixels[base + 1] = odd_next * ahead + (1.0 - odd_next) * imgs[2, 1].astype(F32)

        for i in range(2):
            encode(2 + base + i, pixels.at[base + i])
        for anchor in range(3):
            for i in range(2):
                aspec[base + i, anchor] = spectrum(2 + base + i, anchor)

    step(0)
    for name in ("flag", "cot_s"):
        copies[name].wait_recv()

    @pl.when(sec == 0)
    def _():
        cots[0, 1:3] = jnp.zeros((2, 2, SIDE, SIDE), BF16)

    def prior_cots(index):
        cot_pair(0, index + 1)

    for index in range(2):
        prior_cots(index)
    step(1)
    copies["cot_d"].wait_recv()

    @pl.when(sec == 0)
    def _():
        cots[0, 0] = jnp.zeros((2, SIDE, SIDE), BF16)

    cot_pair(0, 0)

    prior = 2 - 2 * core
    later = 2 * core

    def finish(anchor):
        came_next = flag_in[0:1, 0:1]
        came_after = flag_in[1:2, 0:1]
        k_re, k_im = kernel_of(0, anchor, 1)
        last_re, last_im = plain_product(k_re, k_im, aspec[prior + 1, anchor])
        k_re, k_im = kernel_of(0, anchor, 0)
        p_re, p_im = plain_product(came_after * k_re, came_after * k_im, aspec[prior, anchor])
        g_re = p_re + came_next * last_re
        g_im = p_im + came_next * last_im
        h_re = gspec[anchor, 0:SIDE] + (1.0 - came_next) * last_re
        h_im = gspec[anchor, SIDE:] + (1.0 - came_next) * last_im
        k_re, k_im = kernel_of(1, anchor, 0)
        p_re, p_im = conj_product(k_re, k_im, aspec[later, anchor])
        g_re, g_im = g_re + p_re, g_im + p_im
        k_re, k_im = kernel_of(1, anchor, 1)
        p_re, p_im = conj_product(k_re, k_im, aspec[later + 1, anchor])
        h_re, h_im = h_re + p_re, h_im + p_im
        for member, (re, im) in enumerate(((g_re, g_im), (h_re, h_im))):
            half = left_dot(w_high(), w_low(), jnp.concatenate([re, im], axis=0))
            back = right_dot(regroup(half), v_high(), v_low())
            for c in range(4):
                q, part = c // 2, c % 2
                slope = back[q * SIDE : (q + 1) * SIDE, part * SIDE : (part + 1) * SIDE]
                slope = slope * (0.25 / (SIDE * SIDE))
                unit, scale = normal(member, anchor, c)
                along = total(slope * unit)
                start = anchor * STEP
                gacc[member, c, pl.ds(start, SIDE), :] += scale * (slope - unit * along)

    def weight_steps(member, half):
        start = STEP + half * STEP
        slopes = []
        for c in range(4):
            values = feat[member, c, pl.ds(start, STEP), :]
            slope = gacc[member, c, pl.ds(start, STEP), :] * (1.0 - values * values)
            slopes.append(slope)
            acc[10 * c + 9] += jnp.sum(slope.reshape(STEP // 8, 8, SIDE), axis=0)
        for u in range(3):
            for v in range(3):
                shifted = shifts[member, v, pl.ds(start + u, STEP), :]
                for c in range(4):
                    part = slopes[c] * shifted
                    acc[10 * c + 3 * u + v] += jnp.sum(part.reshape(STEP // 8, 8, SIDE), axis=0)

    finish(0)
    finish(1)
    weight_steps(0, 0)
    weight_steps(1, 0)
    finish(2)
    results = [
        pltpu.make_async_copy(
            gacc.at[member, :, middle], grad_out.at[member], out_sem.at[member]
        )
        for member in range(2)
    ]
    for result in results:
        result.start()

    weight_steps(0, 1)
    weight_steps(1, 1)
    place = lax.broadcasted_iota(jnp.int32, (1, SIDE), 1)
    mine = jnp.zeros((1, SIDE), F32)
    for index in range(40):
        mine = mine + jnp.where(place == index, total(acc[index]), 0.0)
    for stage in range(2):
        spot = spots[stage]
        ring[stage, spot] = mine
        moves = []
        for d in range(1, sizes[stage]):
            copy = pltpu.make_async_remote_copy(
                src_ref=ring.at[stage, spot],
                dst_ref=ring.at[stage, spot],
                send_sem=ring_send.at[stage, d],
                recv_sem=ring_recv.at[stage, d],
                device_id=rings[stage][d - 1],
                device_id_type=MESH,
            )
            copy.start()
            moves.append(copy)
        for copy in moves:
            copy.wait_recv()
        mine = jnp.sum(ring[stage, 0 : sizes[stage]], axis=0)
        for copy in moves:
            copy.wait_send()
    sums_out[...] = mine
    for copy in copies.values():
        copy.wait_send()
    for result in results:
        result.wait()


def deliver(grad_ref, sums_ref, grad_out, wgrad_out, bgrad_out):
    grad_out[...] = grad_ref[...]
    sums = jnp.broadcast_to(sums_ref[...], (8, SIDE))
    row = lax.broadcasted_iota(jnp.int32, (8, SIDE), 0)
    place = lax.broadcasted_iota(jnp.int32, (8, SIDE), 1)
    taps = jnp.zeros((8, SIDE), F32)
    biases = jnp.zeros((8, SIDE), F32)
    for c in range(4):
        moved = pltpu.roll(sums, (SIDE - 10 * c) % SIDE, 1)
        taps = jnp.where(row == c, moved, taps)
        moved = pltpu.roll(sums, (SIDE - 10 * c - 9 + c) % SIDE, 1)
        biases = jnp.where(place == c, moved, biases)
    wgrad_out[...] = taps[0:4, 0:9]
    bgrad_out[...] = biases[0:1, 0:4]


def on_device(shape, images, pair_skip, patch_mask, cotangent, conv_weight, conv_bias):
    hbm = pl.BlockSpec(memory_space=pl.ANY)
    vmem = pl.BlockSpec(memory_space=pltpu.VMEM)
    wide = max(shape[0] * shape[2], shape[1] * shape[3])
    held = pl.BlockSpec(memory_space=pltpu.HBM)
    member = pl.BlockSpec((1, 4, SIDE, SIDE), lambda i: (i, 0, 0, 0))
    grad, sums = pl.pallas_call(
        functools.partial(kernel, shape),
        out_shape=(
            jax.ShapeDtypeStruct((2, 4, SIDE, SIDE), F32),
            jax.ShapeDtypeStruct((1, SIDE), F32),
        ),
        in_specs=[held] * 7,
        out_specs=(hbm, vmem),
        scratch_shapes=[
            pltpu.SMEM((2,), jnp.int32),
            pltpu.SMEM((2, 2), jnp.int32),
            pltpu.SMEM((4, 9), F32),
            pltpu.SMEM((4,), F32),
            pltpu.VMEM((2, 2, SIDE, SIDE), BF16),
            pltpu.VMEM((4, 2 * SIDE, 2 * SIDE), BF16),
            pltpu.VMEM((3, 2, EXT, SIDE), BF16),
            pltpu.VMEM((2, 3, 2, SIDE, SIDE), BF16),
            pltpu.VMEM((8, SIDE), F32),
            pltpu.VMEM((8, SIDE), F32),
            pltpu.VMEM((6 * SIDE, 4 * SIDE), BF16),
            pltpu.VMEM((4, EXT, SIDE), F32),
            pltpu.VMEM((2, 3, EXT, SIDE), F32),
            pltpu.VMEM((6, 4, 4 * STEP, SIDE), F32),
            pltpu.VMEM((6, 4, 8, SIDE), F32),
            pltpu.VMEM((2, 3, 2 * SIDE, 2 * SIDE), F32),
            pltpu.VMEM((3, 2 * SIDE, 2 * SIDE), F32),
            pltpu.VMEM((4, 3, 2 * SIDE, 2 * SIDE), F32),
            pltpu.VMEM((2, 4, 4 * STEP, SIDE), F32),
            pltpu.VMEM((40, 8, SIDE), F32),
            pltpu.VMEM((2, wide, 1, SIDE), F32),
            pltpu.SemaphoreType.DMA((7,)),
            pltpu.SemaphoreType.DMA((2,)),
            pltpu.SemaphoreType.DMA((12,)),
            pltpu.SemaphoreType.DMA((12,)),
            pltpu.SemaphoreType.DMA((2, wide)),
            pltpu.SemaphoreType.DMA((2, wide)),
        ],
        compiler_params=pltpu.CompilerParams(
            collective_id=0, has_side_effects=True, vmem_limit_bytes=63 * 1024 * 1024
        ),
    )(
        images[:, 0],
        cotangent[:, 0],
        jnp.asarray(dft_constants()),
        pair_skip,
        patch_mask[:, 0],
        conv_weight,
        conv_bias,
    )
    grad, weight_grad, bias_grad = pl.pallas_call(
        deliver,
        grid=(2,),
        out_shape=(
            jax.ShapeDtypeStruct((2, 4, SIDE, SIDE), F32),
            jax.ShapeDtypeStruct((4, 9), F32),
            jax.ShapeDtypeStruct((1, 4), F32),
        ),
        in_specs=[member, vmem],
        out_specs=(member, vmem, vmem),
    )(grad, sums)
    return grad[:, None], weight_grad, bias_grad[0]


def solution(mesh):
    n_sec, n_tile = mesh.shape["sec"], mesh.shape["tile"]
    sizes = {64: (4, 2, 8), 4: (1, 2, 2)}.get(n_tile, (1, 1, n_tile))
    return jax.shard_map(
        functools.partial(on_device, (n_sec, *sizes)),
        mesh=mesh,
        in_specs=(
            P("sec", "tile", None, None),
            P("sec"),
            P("sec", "tile", None),
            P("sec", "tile", None, None, None),
            P(),
            P(),
        ),
        out_specs=(P("sec", "tile", None, None, None), P(), P()),
        check_vma=False,
    )
```
